32 devices in a mesh: dp: 8 (over z, y), mp: 4 (over x, core).
Axes of the slice: x: 2, y: 2, z: 4, core: 2. Of those that a mesh axis runs over, the one named last changes fastest.
Arguments:
- tokens: bfloat16 [8192, 8192], P('dp', 'mp'), may hold values from -6 to 6
- cotangent: bfloat16 [8192, 8192], P('dp', 'mp'), may hold values from -6 to 6
- first_factor: bfloat16 [64, 128, 128], P('mp'), may hold values from -0.5 to 0.5
- second_factor: bfloat16 [64, 128, 128], P('mp'), may hold values from -0.5 to 0.5
Outputs:
- output: bfloat16 [8192, 8192], P('dp', 'mp')
- input_grad: bfloat16 [8192, 8192], P('dp', 'mp')
- first_grad: float32 [64, 128, 128], P('mp')
- second_grad: float32 [64, 128, 128], P('mp')
The draws below stay inside these ranges and needn't reach their ends.
All inputs are finite; a program needn't handle non-finite values.
Results may differ from the reference program's by a relative error of at most 0.007.
Values may be sent and summed in bfloat16 or wider, within the bound.
No kernel may reach another device: no remote copies, remote signals or barrier semaphores. Data moves between devices by JAX's collectives and lax.ppermute only.
A program may use at most 128 MiB of HBM per device.

```python
import jax
import jax.numpy as jnp
from jax import lax

NBLK = 64
BLK = 128
TOK_DEV = 1024
D = 8192
TOKENS = 8192
N_DP = 8


def block_levels(own_key, shape, shards, smallest, largest):
    loudness, own = 1.0, jax.random.fold_in(own_key, 6)
    for position, shards_of in shards:
        draws = jnp.exp(jax.random.uniform(jax.random.fold_in(own, position), (shards_of,), jnp.float32, smallest / len(shards), largest / len(shards)))
        loudness = loudness * jnp.repeat(draws, shape[position] // shards_of).reshape([-1 if axis == position else 1 for axis in range(len(shape))])
    return loudness


def scatter_about(rng, extent, deviation, limit, split=(), held_as=jnp.bfloat16):
    gain = block_levels(rng, extent, split, -0.22, 0.18) if split else 1.0
    values = jax.random.normal(rng, extent, jnp.float32) * deviation * gain
    return jnp.minimum(jnp.maximum(values, -limit), limit).astype(held_as)


def setup_inputs(seed: int = 0) -> dict:
    splits = jax.random.split(jax.random.key(seed), 5)
    tokens = scatter_about(splits[0], (TOKENS, D), 1.0, 6.0, ((0, 8), (1, 4)))
    cotangent = scatter_about(splits[1], (TOKENS, D), 1.0, 6.0, ((0, 8), (1, 4)))
    first_factor = scatter_about(splits[2], (NBLK, BLK, BLK), BLK ** -0.5, 0.5, ((0, 4),))
    second_factor = scatter_about(splits[3], (NBLK, BLK, BLK), BLK ** -0.5, 0.5, ((0, 4),))
    return dict(tokens=tokens, cotangent=cotangent, first_factor=first_factor, second_factor=second_factor)


def mult(form, left, right):
    return jnp.einsum(form, left.astype(jnp.float32), right.astype(jnp.float32), precision=lax.Precision.HIGHEST)

def reference(tokens, cotangent, first_factor, second_factor):
    ratio = BLK // NBLK
    w_first = first_factor.reshape(NBLK, BLK, NBLK, ratio)
    w_second = second_factor.reshape(NBLK, ratio, NBLK, NBLK, ratio)
    xs = tokens.reshape(N_DP, TOK_DEV, NBLK, BLK)
    gs = cotangent.reshape(N_DP, TOK_DEV, NBLK, BLK)

    def block(carry, pair):
        acc_first, acc_second = carry
        xb, gb = pair
        rows = xb.shape[0]
        hidden = mult('nix,ixjc->nijc', xb, w_first).astype(jnp.bfloat16)
        mixed = mult('nijc,jciab->najb', hidden, w_second).astype(jnp.bfloat16)
        zed = mixed.reshape(rows, NBLK, BLK).astype(jnp.float32)
        xf = xb.astype(jnp.float32)
        gf = gb.astype(jnp.float32)
        sig = jax.nn.sigmoid(xf)
        silu = xf * sig
        output = (zed * silu).astype(jnp.bfloat16)
        grad_z = (gf * silu).astype(jnp.bfloat16)
        gate_grad = (gf * zed * sig * (1.0 + xf * (1.0 - sig))).astype(jnp.bfloat16)
        grad_mixed = grad_z.reshape(rows, NBLK, NBLK, ratio)
        acc_second = acc_second + mult('nijc,najb->jciab', hidden, grad_mixed)
        grad_u = mult('najb,jciab->nijc', grad_mixed, w_second).astype(jnp.bfloat16)
        acc_first = acc_first + mult('nix,nijc->ixjc', xb, grad_u)
        input_grad = (mult('nijc,ixjc->nix', grad_u, w_first) + gate_grad.astype(jnp.float32)).astype(jnp.bfloat16)
        return ((acc_first, acc_second), (output, input_grad))
    start = (jnp.zeros((NBLK, BLK, NBLK, ratio), jnp.float32), jnp.zeros((NBLK, ratio, NBLK, NBLK, ratio), jnp.float32))
    (acc_first, acc_second), (outs, grads) = lax.scan(block, start, (xs, gs))
    scale = 1.0 / jnp.sqrt(jnp.float32(TOKENS))
    first_grad = acc_first.reshape(NBLK, BLK, BLK) * scale
    second_grad = acc_second.reshape(NBLK, BLK, BLK) * scale
    return (outs.reshape(TOKENS, D), grads.reshape(TOKENS, D), first_grad, second_grad)
```

```python
import functools

import jax
import jax.numpy as jnp
from jax import lax
from jax.experimental import pallas as pl
from jax.experimental.pallas import tpu as pltpu
from jax.sharding import PartitionSpec as P

BF16, F32 = jnp.bfloat16, jnp.float32
SMEM = pl.BlockSpec(memory_space=pltpu.SMEM)
VMEM_LIMIT = 16 * 2**20
SPAN = 256
GROUP = 256


class Plan:
    def __init__(self, rows, nloc, blk, groups):
        self.rows, self.nloc, self.blk, self.groups = rows, nloc, blk, groups
        self.ratio = blk // (nloc * groups)
        self.piece = self.ratio * nloc
        self.wire = nloc * self.piece
        self.tile = GROUP // nloc
        self.ngroup = nloc * blk // GROUP
        self.span = min(SPAN, rows)


def iotas(size):
    return (
        lax.broadcasted_iota(jnp.int32, (size, size), 0),
        lax.broadcasted_iota(jnp.int32, (size, size), 1),
    )


def onehot(mask):
    return jnp.where(mask, 1.0, 0.0).astype(BF16)


def relative(plan, me):
    r, c = iotas(plan.blk)
    return onehot((r ^ c) == me * plan.piece)


def source_order(plan, me):
    r, c = iotas(plan.blk)
    nblk = plan.nloc * plan.groups
    return onehot(c == (r & (plan.ratio - 1)) * nblk + ((r // plan.ratio) ^ (me * plan.nloc)))


def regroup(plan, back):
    r, c = iotas(GROUP)
    if back:
        r, c = c, r
    return onehot(
        c
        == ((r & (plan.tile - 1)) // plan.ratio) * plan.piece
        + (r // plan.tile) * plan.ratio
        + (r & (plan.ratio - 1))
    )


def dot(a, b, dims):
    return lax.dot_general(a, b, (dims, ((), ())), preferred_element_type=F32)


NN, NT, TN = ((1,), (0,)), ((1,), (1,)), ((0,), (0,))


def join(parts):
    return parts[0] if len(parts) == 1 else jnp.concatenate(parts, axis=0)


def scatter(plan, value, outs, block):
    piece = plan.piece
    at = slice(block * piece, (block + 1) * piece)
    for e in range(plan.groups):
        part = value[e * piece : (e + 1) * piece].astype(BF16)
        outs[e][at, :] = part


def gather(plan, refs, block):
    piece = plan.piece
    parts = []
    for ref in refs:
        part = ref[block * piece : (block + 1) * piece, :]
        parts.append(part if piece % 16 == 0 else part.astype(F32))
    return jnp.concatenate(parts, axis=0).astype(BF16)


def params(count=1):
    return pltpu.CompilerParams(
        dimension_semantics=("arbitrary",) * count, vmem_limit_bytes=VMEM_LIMIT
    )


def cost(flops, moved):
    return pl.CostEstimate(flops=int(flops), bytes_accessed=int(moved), transcendentals=0)


def sends(plan, size, step):
    shapes = [jax.ShapeDtypeStruct((plan.wire, size), BF16)] * plan.groups
    return shapes, arrivals(plan, size, step)


def arrivals(plan, size, step, inside=0):
    at = inside // size
    return [pl.BlockSpec((step * plan.piece, size), lambda i: (i, at))] * plan.groups


def call(kernel, args, in_specs, after=(), into=None, **kwargs):
    count = len(args)
    if into is not None:
        after = [into, *after]
        kwargs["input_output_aliases"] = {count: 0}
    extra = len(after)

    def body(*refs):
        kernel(*refs[:count], *refs[count + extra :])

    return pl.pallas_call(
        body,
        in_specs=list(in_specs) + [pl.BlockSpec(memory_space=pl.ANY)] * extra,
        **kwargs,
    )(*args, *after)


def hold(arrays, after):
    count = len(arrays)
    anywhere = pl.BlockSpec(memory_space=pl.ANY)
    return pl.pallas_call(
        lambda *refs: None,
        out_shape=[pltpu.HBM(a.shape, a.dtype) for a in arrays],
        in_specs=[anywhere] * (count + len(after)),
        out_specs=[anywhere] * count,
        input_output_aliases={i: i for i in range(count)},
        name="hold",
    )(*arrays, *after)


def prepare(plan, me, first, second, after=()):
    def kernel(me_ref, f_ref, s_ref, ft_ref, s_out, st_out):
        rel = relative(plan, me_ref[0])
        order = source_order(plan, me_ref[0])
        for i in range(plan.nloc):
            ft_ref[i] = dot(rel, f_ref[i], NT).astype(BF16)
            rows = dot(order, s_ref[i], NN).astype(BF16)
            s_out[i] = dot(rows, rel, NN).astype(BF16)
            st_out[i] = dot(rel, rows, NT).astype(BF16)

    shape = jax.ShapeDtypeStruct(first.shape, BF16)
    return call(
        kernel,
        (me, first, second),
        [SMEM] + [pl.BlockSpec(memory_space=pltpu.VMEM)] * 2,
        after,
        out_shape=[shape] * 3,
        out_specs=[pl.BlockSpec(memory_space=pltpu.VMEM)] * 3,
        compiler_params=pltpu.CompilerParams(vmem_limit_bytes=VMEM_LIMIT),
        cost_estimate=cost(8 * plan.nloc * plan.blk**3, 5 * first.size * 2),
        name="prepare_factors",
    )


def send_grad_z(plan, me, tokens, cotangent, start, size, after=()):
    step = min(4, plan.nloc)
    shapes, specs = sends(plan, size, step)

    def kernel(me_ref, x_ref, g_ref, *outs):
        rel = relative(plan, me_ref[0])
        for i in range(step):
            cols = slice(i * plan.blk, (i + 1) * plan.blk)
            xf = x_ref[:, cols].astype(F32)
            silu = xf * jax.nn.sigmoid(xf)
            grad_z = (g_ref[:, cols].astype(F32) * silu).astype(BF16)
            scatter(plan, dot(rel, grad_z, NT), outs, i)

    block = pl.BlockSpec((size, step * plan.blk), lambda i: (start // size, i))
    return call(
        kernel,
        (me, tokens, cotangent),
        [SMEM, block, block],
        after,
        grid=(plan.nloc // step,),
        out_shape=shapes,
        out_specs=specs,
        compiler_params=params(),
        cost_estimate=cost(2 * size * plan.nloc * plan.blk**2, 6 * size * plan.nloc * plan.blk),
        name="send_grad_z",
    )


def send_hidden(plan, tokens, first_t, start, size, after=()):
    step = min(4, plan.nloc)
    shapes, specs = sends(plan, size, step)

    def kernel(x_ref, w_ref, *outs):
        for i in range(step):
            cols = slice(i * plan.blk, (i + 1) * plan.blk)
            scatter(plan, dot(w_ref[i], x_ref[:, cols], NT), outs, i)

    return call(
        kernel,
        (tokens, first_t),
        [
            pl.BlockSpec((size, step * plan.blk), lambda i: (start // size, i)),
            pl.BlockSpec((step, plan.blk, plan.blk), lambda i: (i, 0, 0)),
        ],
        after,
        grid=(plan.nloc // step,),
        out_shape=shapes,
        out_specs=specs,
        compiler_params=params(),
        cost_estimate=cost(2 * size * plan.nloc * plan.blk**2, 4 * size * plan.nloc * plan.blk),
        name="send_hidden",
    )


def to_blocks(plan, refs, out):
    matrix = regroup(plan, False)
    for g in range(plan.ngroup):
        begin, parts = g * GROUP, []
        while begin < (g + 1) * GROUP:
            e, inside = begin // plan.wire, begin % plan.wire
            take = min(plan.wire - inside, (g + 1) * GROUP - begin)
            parts.append(refs[e][inside : inside + take, :])
            begin += take
        moved = dot(matrix, join(parts), NN).astype(BF16)
        for j in range(plan.nloc):
            out[j, g * plan.tile : (g + 1) * plan.tile, :] = moved[
                j * plan.tile : (j + 1) * plan.tile
            ]


def from_blocks(plan, held, outs):
    matrix = regroup(plan, True)
    for g in range(plan.ngroup):
        rows = join([held[j, g * plan.tile : (g + 1) * plan.tile, :] for j in range(plan.nloc)])
        moved = dot(matrix, rows, NN).astype(BF16)
        begin = g * GROUP
        while begin < (g + 1) * GROUP:
            e, inside = begin // plan.wire, begin % plan.wire
            take = min(plan.wire - inside, (g + 1) * GROUP - begin)
            part = moved[begin - g * GROUP : begin - g * GROUP + take]
            at = slice(inside, inside + take)
            outs[e][at, :] = part
            begin += take


def whole_spec(shape):
    return pl.BlockSpec(shape, lambda i: (0,) * len(shape))


def own_grad_mixed(plan, arrived, size, after=()):
    count = len(arrived)
    kept = (plan.nloc, plan.blk, size)

    def kernel(*refs):
        to_blocks(plan, refs[:count], refs[count])

    return call(
        kernel,
        list(arrived),
        arrivals(plan, size, plan.nloc),
        after,
        grid=(1,),
        out_shape=pltpu.VMEM(kept, BF16),
        out_specs=whole_spec(kept),
        compiler_params=params(),
        cost_estimate=cost(
            4 * size * plan.nloc * plan.blk**2, 4 * size * plan.nloc * plan.blk
        ),
        name="own_grad_mixed",
    )


def own_u(plan, me, arrived, grad_mixed, total, into, start, size, scale, after=()):
    count = len(arrived)
    kept = (plan.nloc, plan.blk, size)
    square = (plan.nloc, plan.blk, plan.blk)
    extra = [] if total is None else [total]

    def kernel(*refs):
        me_ref, ins, g_ref = refs[0], refs[1 : 1 + count], refs[1 + count]
        u_ref, sum_ref = refs[-2:]
        to_blocks(plan, ins, u_ref)
        if scale is not None:
            rel, order = relative(plan, me_ref[0]), source_order(plan, me_ref[0])
        for j in range(plan.nloc):
            term = dot(u_ref[j], g_ref[j], NT)
            if extra:
                term = term + refs[2 + count][j]
            if scale is not None:
                term = term * scale
                high = term.astype(BF16)
                low = (term - high.astype(F32)).astype(BF16)
                high = dot(dot(order, high, TN).astype(BF16), rel, NN)
                term = high + dot(dot(order, low, TN).astype(BF16), rel, NN)
            sum_ref[j] = term

    return call(
        kernel,
        [me] + list(arrived) + [grad_mixed] + extra,
        [SMEM]
        + arrivals(plan, size, plan.nloc)
        + [whole_spec(kept)]
        + [whole_spec(square)] * len(extra),
        after,
        into,
        grid=(1,),
        out_shape=[
            pltpu.HBM((plan.nloc, plan.blk, plan.rows), BF16),
            jax.ShapeDtypeStruct(square, F32),
        ],
        out_specs=[
            pl.BlockSpec(kept, lambda i: (0, 0, start // size)),
            whole_spec(square),
        ],
        compiler_params=params(),
        cost_estimate=cost(
            6 * size * plan.nloc * plan.blk**2, 6 * size * plan.nloc * plan.blk
        ),
        name="own_u",
    )


def own_product(plan, u, factor, name, start, size, after=()):
    span = plan.span
    shapes, _ = sends(plan, size, plan.nloc)
    shape = (plan.nloc, plan.blk, span)

    def kernel(u_ref, w_ref, *refs):
        outs, held = refs[:-1], refs[-1]
        for j in range(plan.nloc):
            held[j] = dot(w_ref[j], u_ref[j], NN).astype(BF16)
        from_blocks(plan, held, outs)

    return call(
        kernel,
        (u, factor),
        [pl.BlockSpec(shape, lambda t: (0, 0, t + start // span)), whole_spec(factor.shape)],
        after,
        grid=(size // span,),
        out_shape=shapes,
        out_specs=[pl.BlockSpec((plan.wire, span), lambda t: (0, t))] * plan.groups,
        scratch_shapes=[pltpu.VMEM(shape, BF16)],
        compiler_params=params(),
        cost_estimate=cost(
            6 * size * plan.nloc * plan.blk**2, 4 * size * plan.nloc * plan.blk
        ),
        name=name,
    )


def first_term(plan, me, arrived, tokens, total, start, size, scale, after=()):
    count = len(arrived)
    step = min(4, plan.nloc)
    square = pl.BlockSpec((step, plan.blk, plan.blk), lambda i: (i, 0, 0))
    extra = [] if total is None else [total]

    def kernel(*refs):
        me_ref, ins, x_ref, sum_ref = refs[0], refs[1 : 1 + count], refs[1 + count], refs[-1]
        rel = relative(plan, me_ref[0])
        for i in range(step):
            cols = slice(i * plan.blk, (i + 1) * plan.blk)
            term = dot(gather(plan, ins, i), x_ref[:, cols], NN)
            if extra:
                term = term + refs[2 + count][i]
            if scale is not None:
                term = dot((term * scale).astype(BF16), rel, TN)
            sum_ref[i] = term.astype(sum_ref.dtype)

    return call(
        kernel,
        [me] + list(arrived) + [tokens] + extra,
        [SMEM]
        + arrivals(plan, size, step)
        + [pl.BlockSpec((size, step * plan.blk), lambda i: (start // size, i))]
        + [square] * len(extra),
        after,
        grid=(plan.nloc // step,),
        out_shape=jax.ShapeDtypeStruct(
            (plan.nloc, plan.blk, plan.blk), F32 if scale is None else BF16
        ),
        out_specs=square,
        compiler_params=params(),
        cost_estimate=cost(2 * size * plan.nloc * plan.blk**2, 4 * size * plan.nloc * plan.blk),
        name="first_term",
    )


def gate(plan, me, mixed, inside, grads, tokens, cotangent, first_t, held, start, size, after=()):
    count = len(mixed)
    step = min(4, plan.nloc)
    extra = [] if held is None else list(held)

    def kernel(*refs):
        me_ref, zs, hs = refs[0], refs[1 : 1 + count], refs[1 + count : 1 + 2 * count]
        x_ref, g_ref, w_ref = refs[1 + 2 * count : 4 + 2 * count]
        out_ref, grad_ref, done_ref = refs[-3:]
        done_ref[...] = jnp.zeros_like(done_ref)
        rel = relative(plan, me_ref[0])
        for i in range(step):
            cols = slice(i * plan.blk, (i + 1) * plan.blk)
            zf = dot(gather(plan, zs, i), rel, TN)
            back = dot(gather(plan, hs, i), w_ref[i], TN)
            xf = x_ref[:, cols].astype(F32)
            gf = g_ref[:, cols].astype(F32)
            sig = jax.nn.sigmoid(xf)
            out_ref[:, cols] = (zf * (xf * sig)).astype(BF16)
            gate_grad = (gf * zf * sig * (1.0 + xf * (1.0 - sig))).astype(BF16)
            grad_ref[:, cols] = (back + gate_grad.astype(F32)).astype(BF16)

    block = pl.BlockSpec((size, step * plan.blk), lambda i: (start // size, i))
    shape = pltpu.HBM(tokens.shape, BF16)
    before = 4 + 2 * count
    return call(
        kernel,
        [me] + list(mixed) + list(grads) + [tokens, cotangent, first_t] + extra,
        [SMEM]
        + arrivals(plan, size, step, inside)
        + arrivals(plan, size, step)
        + [block, block, pl.BlockSpec((step, plan.blk, plan.blk), lambda i: (i, 0, 0))]
        + [pl.BlockSpec(memory_space=pl.ANY)] * len(extra),
        after,
        grid=(plan.nloc // step,),
        out_shape=[shape, shape, jax.ShapeDtypeStruct((8, 128), F32)],
        out_specs=[block, block, whole_spec((8, 128))],
        input_output_aliases={before: 0, before + 1: 1} if extra else {},
        compiler_params=params(),
        cost_estimate=cost(
            4 * size * plan.nloc * plan.blk**2, 12 * size * plan.nloc * plan.blk
        ),
        name="gate",
    )


def reorder(kernel, args, shapes, name, after=()):
    vmem = pl.BlockSpec(memory_space=pltpu.VMEM)
    moved = sum(a.size for a in args) * 2
    return call(
        kernel,
        args,
        [SMEM] + [vmem] * (len(args) - 1),
        after,
        out_shape=shapes,
        out_specs=[vmem] * len(shapes),
        compiler_params=pltpu.CompilerParams(vmem_limit_bytes=VMEM_LIMIT),
        cost_estimate=cost(moved, 2 * moved),
        name=name,
    )


def halves(place, total, after=()):
    rows, cols = total.shape
    half = rows // 2

    def kernel(place_ref, t_ref, keep_ref, send_ref):
        side = place_ref[0] & 1
        keep_ref[...] = t_ref[pl.ds(pl.multiple_of(side * half, half), half), :]
        send_ref[...] = t_ref[pl.ds(pl.multiple_of((1 - side) * half, half), half), :]

    return reorder(
        kernel, (place, total), [jax.ShapeDtypeStruct((half, cols), BF16)] * 2, "halves", after
    )


def quarters(place, keep, got, count, after=()):
    rows, cols = keep.shape
    part = rows // count

    def kernel(place_ref, a_ref, b_ref, *outs):
        for e in range(count):
            at = pl.multiple_of(((place_ref[0] >> 1) ^ e) * part, part)
            value = a_ref[pl.ds(at, part), :].astype(F32) + b_ref[pl.ds(at, part), :].astype(F32)
            outs[e][...] = value.astype(outs[e].dtype)

    shapes = [jax.ShapeDtypeStruct((part, cols), BF16 if e else F32) for e in range(count)]
    return reorder(kernel, (place, keep, got), shapes, "quarters", after)


def add_up(place, own, others, after=()):
    def kernel(place_ref, own_ref, *refs):
        value = own_ref[...]
        for ref in refs[:-1]:
            value = value + ref[...].astype(F32)
        refs[-1][...] = value.astype(BF16)

    shape = jax.ShapeDtypeStruct(own.shape, BF16)
    return reorder(kernel, (place, own, *others), [shape], "add_up", after)[0]


def join_parts(place, parts, after=()):
    count = len(parts)
    part, cols = parts[0].shape

    def kernel(place_ref, *refs):
        for e in range(count):
            at = pl.multiple_of(((place_ref[0] >> 1) ^ e) * part, part)
            refs[-1][pl.ds(at, part), :] = refs[e][...]

    shape = jax.ShapeDtypeStruct((part * count, cols), BF16)
    return reorder(kernel, (place, *parts), [shape], "join_parts", after)[0]


def join_halves(place, mine, other, after=()):
    half, cols = mine.shape

    def kernel(place_ref, m_ref, o_ref, out_ref):
        side = place_ref[0] & 1
        out_ref[pl.ds(pl.multiple_of(side * half, half), half), :] = m_ref[...].astype(F32)
        out_ref[pl.ds(pl.multiple_of((1 - side) * half, half), half), :] = o_ref[...].astype(F32)

    shape = jax.ShapeDtypeStruct((2 * half, cols), F32)
    return reorder(kernel, (place, mine, other), [shape], "join_halves", after)[0]


def swap(value, by, axis, size):
    return lax.ppermute(value, axis, [(i, i ^ by) for i in range(size)])


def shards(tokens, cotangent, first_factor, second_factor):
    nloc, blk, _ = first_factor.shape
    plan = Plan(tokens.shape[0], nloc, blk, lax.axis_size("mp"))
    rows, parts = plan.rows, lax.axis_size("dp")
    size = plan.span
    chunks = [(start, size) for start in range(0, rows, size)]
    count = len(chunks)
    me = lax.axis_index("mp").astype(jnp.int32).reshape(1)
    scale = float((rows * parts) ** -0.5)
    tokens = pltpu.with_memory_space_constraint(tokens, pltpu.HBM)
    cotangent = pltpu.with_memory_space_constraint(cotangent, pltpu.HBM)
    crossed = []
    order = []

    def after(slot=None):
        found = [] if slot is None or slot < 0 else list(crossed[slot])
        return found + order[-1:]

    def ran(result):
        order.append(result[0] if isinstance(result, (list, tuple)) else result)
        return result

    def send(bufs):
        ran(bufs)
        arrived = [bufs[0]]
        arrived += [swap(v, e, "mp", plan.groups) for e, v in enumerate(bufs[1:], 1)]
        crossed.append(arrived[2:])
        return arrived

    def hbm(arrays):
        return [pltpu.with_memory_space_constraint(a, pltpu.HBM) for a in arrays]

    grad_z, hidden, kept, grad_u, mixed = [], [], [], [], {}
    sums = dict(first=None, second=None, held=None, u=None)
    last = [None] * (count - 1) + [scale]

    def do_grad_z(k, slot):
        grad_z.append(send(send_grad_z(plan, me, tokens, cotangent, *chunks[k], after(slot))))

    def do_hidden(k, slot):
        hidden.append(send(send_hidden(plan, tokens, first_t, *chunks[k], after(slot))))

    def do_kept(k):
        kept.append(ran(own_grad_mixed(plan, grad_z[k], chunks[k][1], after())))

    def do_grad_u(k, slot):
        args = (plan, kept[k], second, "own_grad_u", 0, size, after(slot))
        grad_u.append(send(own_product(*args)))

    def do_u(k):
        args = (hidden[k], kept[k], sums["second"], sums["u"], *chunks[k], last[k], after())
        sums["u"], sums["second"] = own_u(plan, me, *args)
        ran(sums["second"])

    def do_first(k):
        args = (hbm(grad_u[k]), tokens, sums["first"], *chunks[k], last[k])
        sums["first"] = ran(first_term(plan, me, *args, after()))

    def do_mixed(start, length):
        args = (plan, sums["u"], second_t, "own_mixed", start, length, after())
        return ran(own_product(*args))

    def send_mixed(bufs, start, length, slot):
        arrived = send(hold(bufs, after(slot)))
        for k in range(count):
            if start <= chunks[k][0] < start + length:
                mixed[k] = (arrived, chunks[k][0] - start)

    def do_gate(k, slot, extra=()):
        arrived, inside = mixed[k]
        args = (hbm(arrived), inside, hbm(grad_u[k]), tokens, cotangent, first_t, sums["held"])
        *held, done = gate(plan, me, *args, *chunks[k], after(slot) + list(extra))
        sums["held"] = held
        ran(done)

    place = lax.axis_index("dp").astype(jnp.int32).reshape(1)
    state = []

    def split(slot):
        total = sums["first"].reshape(nloc * blk, blk)
        state[:] = ran(halves(place, total, after(slot)))
        state[1] = swap(state[1], 1, "dp", parts)

    def reduce(slot):
        state[:] = ran(quarters(place, *state, parts // 2, after(slot)))
        state[1:] = [swap(v, 2 * e, "dp", parts) for e, v in enumerate(state[1:], 1)]

    def add(slot):
        summed = ran(add_up(place, state[0], state[1:], after(slot)))
        state[:] = [summed] + [swap(summed, 2 * e, "dp", parts) for e in range(1, parts // 2)]

    def join(slot):
        mine = ran(join_parts(place, state, after(slot)))
        state[:] = [mine, swap(mine, 1, "dp", parts)]

    def finish(slot):
        state[:] = [ran(join_halves(place, *state[:2], after(slot) + state[2:]))]

    lead = 3
    for k in range(count):
        do_grad_z(k, k - lead)
        if k == min(lead, count) - 1:
            first_t, second, second_t = ran(
                prepare(plan, me, first_factor, second_factor, after())
            )
    for k in range(count):
        do_hidden(k, count + k - lead)
        do_kept(k)
    do_u(0)
    for k in range(count):
        do_grad_u(k, 2 * count + k - lead)
        if k + 1 < count:
            do_u(k + 1)
    second_grad = lax.psum(sums["second"], "dp")
    late = do_mixed(size, rows - size) if count > 1 else None
    early = do_mixed(0, size)
    for k in range(count - 1):
        do_first(k)
    if count > 1:
        send_mixed(late, size, rows - size, 3 * count - 1)
    do_first(count - 1)
    split(None)
    reduce(None)
    send_mixed(early, 0, size, None)
    add(None)
    for k in range(1, count):
        do_gate(k, None, [second_grad] if k == count - 1 else [])
    join(None)
    do_gate(0, None)
    finish(None)
    first_grad = state[0].reshape(nloc, blk, blk)
    held = sums["held"]
    return (held[0], held[1], first_grad, second_grad)


def solution(mesh):
    return jax.shard_map(
        shards,
        mesh=mesh,
        in_specs=(P("dp", "mp"), P("dp", "mp"), P("mp", None, None), P("mp", None, None)),
        out_specs=(P("dp", "mp"), P("dp", "mp"), P("mp", None, None), P("mp", None, None)),
        check_vma=False,
    )
```

```python
import functools

import jax
import jax.numpy as jnp
from jax import lax
from jax.experimental import pallas as pl
from jax.experimental.pallas import tpu as pltpu
from jax.sharding import PartitionSpec as P

BF16, F32 = jnp.bfloat16, jnp.float32
SMEM = pl.BlockSpec(memory_space=pltpu.SMEM)
VMEM_LIMIT = 16 * 2**20
SPAN = 256
GROUP = 256


class Plan:
    def __init__(self, rows, nloc, blk, groups):
        self.rows, self.nloc, self.blk, self.groups = rows, nloc, blk, groups
        self.ratio = blk // (nloc * groups)
        self.piece = self.ratio * nloc
        self.wire = nloc * self.piece
        self.tile = GROUP // nloc
        self.ngroup = nloc * blk // GROUP
        self.span = min(SPAN, rows)


def iotas(size):
    return (
        lax.broadcasted_iota(jnp.int32, (size, size), 0),
        lax.broadcasted_iota(jnp.int32, (size, size), 1),
    )


def onehot(mask):
    return jnp.where(mask, 1.0, 0.0).astype(BF16)


def relative(plan, me):
    r, c = iotas(plan.blk)
    return onehot((r ^ c) == me * plan.piece)


def source_order(plan, me):
    r, c = iotas(plan.blk)
    nblk = plan.nloc * plan.groups
    return onehot(c == (r & (plan.ratio - 1)) * nblk + ((r // plan.ratio) ^ (me * plan.nloc)))


def regroup(plan, back):
    r, c = iotas(GROUP)
    if back:
        r, c = c, r
    return onehot(
        c
        == ((r & (plan.tile - 1)) // plan.ratio) * plan.piece
        + (r // plan.tile) * plan.ratio
        + (r & (plan.ratio - 1))
    )


def dot(a, b, dims):
    return lax.dot_general(a, b, (dims, ((), ())), preferred_element_type=F32)


NN, NT, TN = ((1,), (0,)), ((1,), (1,)), ((0,), (0,))


def sigmoid(x):
    return 0.5 * jnp.tanh(0.5 * x) + 0.5


def in_hbm(array):
    return pltpu.with_memory_space_constraint(array, pltpu.HBM)


def join(parts):
    return parts[0] if len(parts) == 1 else jnp.concatenate(parts, axis=0)


def scatter(plan, value, outs, block):
    piece = plan.piece
    at = slice(block * piece, (block + 1) * piece)
    for e in range(plan.groups):
        part = value[e * piece : (e + 1) * piece].astype(BF16)
        outs[e][at, :] = part


def gather(plan, refs, block):
    piece = plan.piece
    parts = []
    for ref in refs:
        part = ref[block * piece : (block + 1) * piece, :]
        parts.append(part if piece % 16 == 0 else part.astype(F32))
    return jnp.concatenate(parts, axis=0).astype(BF16)


def params(count=1):
    return pltpu.CompilerParams(
        dimension_semantics=("arbitrary",) * count, vmem_limit_bytes=VMEM_LIMIT
    )


def cost(flops, moved):
    return pl.CostEstimate(flops=int(flops), bytes_accessed=int(moved), transcendentals=0)


def sends(plan, size, step):
    shapes = [jax.ShapeDtypeStruct((plan.wire, size), BF16)] * plan.groups
    return shapes, arrivals(plan, size, step)


def arrivals(plan, size, step, inside=0):
    at = inside // size
    return [pl.BlockSpec((step * plan.piece, size), lambda i: (i, at))] * plan.groups


def call(kernel, args, in_specs, after=(), into=None, **kwargs):
    count = len(args)
    if into is not None:
        after = [into, *after]
        kwargs["input_output_aliases"] = {count: 0}
    extra = len(after)

    def body(*refs):
        kernel(*refs[:count], *refs[count + extra :])

    return pl.pallas_call(
        body,
        in_specs=list(in_specs) + [pl.BlockSpec(memory_space=pl.ANY)] * extra,
        **kwargs,
    )(*args, *after)


def hold(arrays, after):
    count = len(arrays)
    anywhere = pl.BlockSpec(memory_space=pl.ANY)
    return pl.pallas_call(
        lambda *refs: None,
        out_shape=[pltpu.HBM(a.shape, a.dtype) for a in arrays],
        in_specs=[anywhere] * (count + len(after)),
        out_specs=[anywhere] * count,
        input_output_aliases={i: i for i in range(count)},
        name="hold",
    )(*arrays, *after)


def prepare(plan, me, first, second, after=()):
    def kernel(me_ref, f_ref, s_ref, ft_ref, s_out, st_out):
        rel = relative(plan, me_ref[0])
        order = source_order(plan, me_ref[0])
        for i in range(plan.nloc):
            ft_ref[i] = dot(rel, f_ref[i], NT).astype(BF16)
            rows = dot(order, s_ref[i], NN).astype(BF16)
            s_out[i] = dot(rows, rel, NN).astype(BF16)
            st_out[i] = dot(rel, rows, NT).astype(BF16)

    shape = jax.ShapeDtypeStruct(first.shape, BF16)
    return call(
        kernel,
        (me, first, second),
        [SMEM] + [pl.BlockSpec(memory_space=pltpu.VMEM)] * 2,
        after,
        out_shape=[shape] * 3,
        out_specs=[pl.BlockSpec(memory_space=pltpu.VMEM)] * 3,
        compiler_params=pltpu.CompilerParams(vmem_limit_bytes=VMEM_LIMIT),
        cost_estimate=cost(8 * plan.nloc * plan.blk**3, 5 * first.size * 2),
        name="prepare_factors",
    )


def send_grad_z(plan, me, tokens, cotangent, start, size, after=()):
    step = min(8, plan.nloc)
    shapes, specs = sends(plan, size, step)

    def kernel(me_ref, x_ref, g_ref, *outs):
        rel = relative(plan, me_ref[0])
        for i in range(step):
            cols = slice(i * plan.blk, (i + 1) * plan.blk)
            xf = x_ref[:, cols].astype(F32)
            silu = xf * sigmoid(xf)
            grad_z = (g_ref[:, cols].astype(F32) * silu).astype(BF16)
            scatter(plan, dot(rel, grad_z, NT), outs, i)

    block = pl.BlockSpec((size, step * plan.blk), lambda i: (start // size, i))
    return call(
        kernel,
        (me, tokens, cotangent),
        [SMEM, block, block],
        after,
        grid=(plan.nloc // step,),
        out_shape=shapes,
        out_specs=specs,
        compiler_params=params(),
        cost_estimate=cost(2 * size * plan.nloc * plan.blk**2, 6 * size * plan.nloc * plan.blk),
        name="send_grad_z",
    )


def send_hidden(plan, tokens, first_t, start, size, after=()):
    step = min(8, plan.nloc)
    shapes, specs = sends(plan, size, step)

    def kernel(x_ref, w_ref, *outs):
        for i in range(step):
            cols = slice(i * plan.blk, (i + 1) * plan.blk)
            scatter(plan, dot(w_ref[i], x_ref[:, cols], NT), outs, i)

    return call(
        kernel,
        (tokens, first_t),
        [
            pl.BlockSpec((size, step * plan.blk), lambda i: (start // size, i)),
            pl.BlockSpec((step, plan.blk, plan.blk), lambda i: (i, 0, 0)),
        ],
        after,
        grid=(plan.nloc // step,),
        out_shape=shapes,
        out_specs=specs,
        compiler_params=params(),
        cost_estimate=cost(2 * size * plan.nloc * plan.blk**2, 4 * size * plan.nloc * plan.blk),
        name="send_hidden",
    )


def to_blocks(plan, refs, out):
    matrix = regroup(plan, False)
    for g in range(plan.ngroup):
        begin, parts = g * GROUP, []
        while begin < (g + 1) * GROUP:
            e, inside = begin // plan.wire, begin % plan.wire
            take = min(plan.wire - inside, (g + 1) * GROUP - begin)
            parts.append(refs[e][inside : inside + take, :])
            begin += take
        moved = dot(matrix, join(parts), NN).astype(BF16)
        for j in range(plan.nloc):
            out[j, g * plan.tile : (g + 1) * plan.tile, :] = moved[
                j * plan.tile : (j + 1) * plan.tile
            ]


def from_blocks(plan, held, outs):
    matrix = regroup(plan, True)
    for g in range(plan.ngroup):
        rows = join([held[j, g * plan.tile : (g + 1) * plan.tile, :] for j in range(plan.nloc)])
        moved = dot(matrix, rows, NN).astype(BF16)
        begin = g * GROUP
        while begin < (g + 1) * GROUP:
            e, inside = begin // plan.wire, begin % plan.wire
            take = min(plan.wire - inside, (g + 1) * GROUP - begin)
            part = moved[begin - g * GROUP : begin - g * GROUP + take]
            at = slice(inside, inside + take)
            outs[e][at, :] = part
            begin += take


def whole_spec(shape):
    return pl.BlockSpec(shape, lambda i: (0,) * len(shape))


def own_grad_mixed(plan, arrived, size, after=()):
    count = len(arrived)
    kept = (plan.nloc, plan.blk, size)

    def kernel(*refs):
        to_blocks(plan, refs[:count], refs[count])

    return call(
        kernel,
        list(arrived),
        arrivals(plan, size, plan.nloc),
        after,
        grid=(1,),
        out_shape=pltpu.VMEM(kept, BF16),
        out_specs=whole_spec(kept),
        compiler_params=params(),
        cost_estimate=cost(
            4 * size * plan.nloc * plan.blk**2, 4 * size * plan.nloc * plan.blk
        ),
        name="own_grad_mixed",
    )


def own_u(plan, me, arrived, grad_mixed, total, into, start, size, scale, after=()):
    count = len(arrived)
    kept = (plan.nloc, plan.blk, size)
    square = (plan.nloc, plan.blk, plan.blk)
    extra = [] if total is None else [total]

    def kernel(*refs):
        me_ref, ins, g_ref = refs[0], refs[1 : 1 + count], refs[1 + count]
        u_ref, sum_ref = refs[-2:]
        to_blocks(plan, ins, u_ref)
        if scale is not None:
            rel, order = relative(plan, me_ref[0]), source_order(plan, me_ref[0])
        for j in range(plan.nloc):
            term = dot(u_ref[j], g_ref[j], NT)
            if extra:
                term = term + refs[2 + count][j]
            if scale is not None:
                term = term * scale
                high = term.astype(BF16)
                low = (term - high.astype(F32)).astype(BF16)
                high = dot(dot(order, high, TN).astype(BF16), rel, NN)
                term = high + dot(dot(order, low, TN).astype(BF16), rel, NN)
            sum_ref[j] = term

    return call(
        kernel,
        [me] + list(arrived) + [grad_mixed] + extra,
        [SMEM]
        + arrivals(plan, size, plan.nloc)
        + [whole_spec(kept)]
        + [whole_spec(square)] * len(extra),
        after,
        into,
        grid=(1,),
        out_shape=[
            pltpu.HBM((plan.nloc, plan.blk, plan.rows), BF16),
            jax.ShapeDtypeStruct(square, F32),
        ],
        out_specs=[
            pl.BlockSpec(kept, lambda i: (0, 0, start // size)),
            whole_spec(square),
        ],
        compiler_params=params(),
        cost_estimate=cost(
            6 * size * plan.nloc * plan.blk**2, 6 * size * plan.nloc * plan.blk
        ),
        name="own_u",
    )


def own_product(plan, u, factor, name, start, size, after=()):
    span = plan.span
    shapes, _ = sends(plan, size, plan.nloc)
    shape = (plan.nloc, plan.blk, span)

    def kernel(u_ref, w_ref, *refs):
        outs, held = refs[:-1], refs[-1]
        for j in range(plan.nloc):
            held[j] = dot(w_ref[j], u_ref[j], NN).astype(BF16)
        from_blocks(plan, held, outs)

    return call(
        kernel,
        (u, in_hbm(factor)),
        [pl.BlockSpec(shape, lambda t: (0, 0, t + start // span)), whole_spec(factor.shape)],
        after,
        grid=(size // span,),
        out_shape=shapes,
        out_specs=[pl.BlockSpec((plan.wire, span), lambda t: (0, t))] * plan.groups,
        scratch_shapes=[pltpu.VMEM(shape, BF16)],
        compiler_params=params(),
        cost_estimate=cost(
            6 * size * plan.nloc * plan.blk**2, 4 * size * plan.nloc * plan.blk
        ),
        name=name,
    )


def first_term(plan, me, arrived, tokens, total, start, size, scale, after=()):
    count = len(arrived)
    step = min(8, plan.nloc)
    square = pl.BlockSpec((step, plan.blk, plan.blk), lambda i: (i, 0, 0))
    extra = [] if total is None else [total]

    def kernel(*refs):
        me_ref, ins, x_ref, sum_ref = refs[0], refs[1 : 1 + count], refs[1 + count], refs[-1]
        rel = relative(plan, me_ref[0])
        for i in range(step):
            cols = slice(i * plan.blk, (i + 1) * plan.blk)
            term = dot(gather(plan, ins, i), x_ref[:, cols], NN)
            if extra:
                term = term + refs[2 + count][i]
            if scale is not None:
                term = dot((term * scale).astype(BF16), rel, TN)
            sum_ref[i] = term.astype(sum_ref.dtype)

    return call(
        kernel,
        [me] + list(arrived) + [tokens] + extra,
        [SMEM]
        + arrivals(plan, size, step)
        + [pl.BlockSpec((size, step * plan.blk), lambda i: (start // size, i))]
        + [square] * len(extra),
        after,
        grid=(plan.nloc // step,),
        out_shape=jax.ShapeDtypeStruct(
            (plan.nloc, plan.blk, plan.blk), F32 if scale is None else BF16
        ),
        out_specs=square,
        compiler_params=params(),
        cost_estimate=cost(2 * size * plan.nloc * plan.blk**2, 4 * size * plan.nloc * plan.blk),
        name="first_term",
    )


def gate(plan, me, mixed, inside, grads, tokens, cotangent, first_t, held, start, size, after=()):
    count = len(mixed)
    step = min(8, plan.nloc)
    extra = [] if held is None else list(held)

    def kernel(*refs):
        me_ref, zs, hs = refs[0], refs[1 : 1 + count], refs[1 + count : 1 + 2 * count]
        x_ref, g_ref, w_ref = refs[1 + 2 * count : 4 + 2 * count]
        out_ref, grad_ref, done_ref = refs[-3:]
        done_ref[...] = jnp.zeros_like(done_ref)
        rel = relative(plan, me_ref[0])
        for i in range(step):
            cols = slice(i * plan.blk, (i + 1) * plan.blk)
            zf = dot(gather(plan, zs, i), rel, TN)
            back = dot(gather(plan, hs, i), w_ref[i], TN)
            xf = x_ref[:, cols].astype(F32)
            gf = g_ref[:, cols].astype(F32)
            sig = sigmoid(xf)
            silu = xf * sig
            out_ref[:, cols] = (zf * silu).astype(BF16)
            gate_grad = (gf * zf * (sig + silu * (1.0 - sig))).astype(BF16)
            grad_ref[:, cols] = (back + gate_grad.astype(F32)).astype(BF16)

    block = pl.BlockSpec((size, step * plan.blk), lambda i: (start // size, i))
    shape = pltpu.HBM(tokens.shape, BF16)
    before = 4 + 2 * count
    return call(
        kernel,
        [me] + list(mixed) + list(grads) + [tokens, cotangent, in_hbm(first_t)] + extra,
        [SMEM]
        + arrivals(plan, size, step, inside)
        + arrivals(plan, size, step)
        + [block, block, pl.BlockSpec((step, plan.blk, plan.blk), lambda i: (i, 0, 0))]
        + [pl.BlockSpec(memory_space=pl.ANY)] * len(extra),
        after,
        grid=(plan.nloc // step,),
        out_shape=[shape, shape, jax.ShapeDtypeStruct((8, 128), F32)],
        out_specs=[block, block, whole_spec((8, 128))],
        input_output_aliases={before: 0, before + 1: 1} if extra else {},
        compiler_params=params(),
        cost_estimate=cost(
            4 * size * plan.nloc * plan.blk**2, 12 * size * plan.nloc * plan.blk
        ),
        name="gate",
    )


def reorder(kernel, args, shapes, name, after=()):
    vmem = pl.BlockSpec(memory_space=pltpu.VMEM)
    moved = sum(a.size for a in args) * 2
    return call(
        kernel,
        args,
        [SMEM] + [vmem] * (len(args) - 1),
        after,
        out_shape=shapes,
        out_specs=[vmem] * len(shapes),
        compiler_params=pltpu.CompilerParams(vmem_limit_bytes=VMEM_LIMIT),
        cost_estimate=cost(moved, 2 * moved),
        name=name,
    )


def halves(place, total, after=()):
    rows, cols = total.shape
    half = rows // 2

    def kernel(place_ref, t_ref, keep_ref, send_ref):
        side = place_ref[0] & 1
        keep_ref[...] = t_ref[pl.ds(pl.multiple_of(side * half, half), half), :]
        send_ref[...] = t_ref[pl.ds(pl.multiple_of((1 - side) * half, half), half), :]

    return reorder(
        kernel, (place, total), [jax.ShapeDtypeStruct((half, cols), BF16)] * 2, "halves", after
    )


def quarters(place, keep, got, count, after=()):
    rows, cols = keep.shape
    part = rows // count

    def kernel(place_ref, a_ref, b_ref, *outs):
        for e in range(count):
            at = pl.multiple_of(((place_ref[0] >> 1) ^ e) * part, part)
            value = a_ref[pl.ds(at, part), :].astype(F32) + b_ref[pl.ds(at, part), :].astype(F32)
            outs[e][...] = value.astype(outs[e].dtype)

    shapes = [jax.ShapeDtypeStruct((part, cols), BF16 if e else F32) for e in range(count)]
    return reorder(kernel, (place, keep, got), shapes, "quarters", after)


def add_up(place, own, others, after=()):
    def kernel(place_ref, own_ref, *refs):
        value = own_ref[...]
        for ref in refs[:-1]:
            value = value + ref[...].astype(F32)
        refs[-1][...] = value.astype(BF16)

    shape = jax.ShapeDtypeStruct(own.shape, BF16)
    return reorder(kernel, (place, own, *others), [shape], "add_up", after)[0]


def join_parts(place, parts, after=()):
    count = len(parts)
    part, cols = parts[0].shape

    def kernel(place_ref, *refs):
        for e in range(count):
            at = pl.multiple_of(((place_ref[0] >> 1) ^ e) * part, part)
            refs[-1][pl.ds(at, part), :] = refs[e][...]

    shape = jax.ShapeDtypeStruct((part * count, cols), BF16)
    return reorder(kernel, (place, *parts), [shape], "join_parts", after)[0]


def join_halves(place, mine, other, after=()):
    half, cols = mine.shape

    def kernel(place_ref, m_ref, o_ref, out_ref):
        side = place_ref[0] & 1
        out_ref[pl.ds(pl.multiple_of(side * half, half), half), :] = m_ref[...].astype(F32)
        out_ref[pl.ds(pl.multiple_of((1 - side) * half, half), half), :] = o_ref[...].astype(F32)

    shape = pltpu.HBM((2 * half, cols), F32)
    return reorder(kernel, (place, mine, other), [shape], "join_halves", after)[0]


def swap(value, by, axis, size):
    return lax.ppermute(value, axis, [(i, i ^ by) for i in range(size)])


def shards(tokens, cotangent, first_factor, second_factor):
    nloc, blk, _ = first_factor.shape
    plan = Plan(tokens.shape[0], nloc, blk, lax.axis_size("mp"))
    rows, parts = plan.rows, lax.axis_size("dp")
    size = plan.span
    chunks = [(start, size) for start in range(0, rows, size)]
    count = len(chunks)
    me = lax.axis_index("mp").astype(jnp.int32).reshape(1)
    scale = float((rows * parts) ** -0.5)
    tokens = pltpu.with_memory_space_constraint(tokens, pltpu.HBM)
    cotangent = pltpu.with_memory_space_constraint(cotangent, pltpu.HBM)
    crossed = []
    order = []

    def after(slot=None):
        found = [] if slot is None or slot < 0 else list(crossed[slot])
        return found + order[-1:]

    def ran(result):
        order.append(result[0] if isinstance(result, (list, tuple)) else result)
        return result

    def send(bufs):
        ran(bufs)
        arrived = [bufs[0]]
        arrived += [swap(v, e, "mp", plan.groups) for e, v in enumerate(bufs[1:], 1)]
        crossed.append(arrived[2:])
        return arrived

    def hbm(arrays):
        return [pltpu.with_memory_space_constraint(a, pltpu.HBM) for a in arrays]

    grad_z, hidden, kept, grad_u, mixed = [], [], [], [], {}
    sums = dict(first=None, second=None, held=None, u=None)
    last = [None] * (count - 1) + [scale]

    def do_grad_z(k, slot):
        grad_z.append(send(send_grad_z(plan, me, tokens, cotangent, *chunks[k], after(slot))))

    def do_hidden(k, slot):
        hidden.append(send(send_hidden(plan, tokens, first_t, *chunks[k], after(slot))))

    def do_kept(k):
        kept.append(ran(own_grad_mixed(plan, grad_z[k], chunks[k][1], after())))

    def do_grad_u(k, slot):
        args = (plan, kept[k], second, "own_grad_u", 0, size, after(slot))
        grad_u.append(send(own_product(*args)))

    def do_u(k):
        args = (hidden[k], kept[k], sums["second"], sums["u"], *chunks[k], last[k], after())
        sums["u"], sums["second"] = own_u(plan, me, *args)
        ran(sums["second"])

    def do_first(k):
        args = (hbm(grad_u[k]), tokens, sums["first"], *chunks[k], last[k])
        sums["first"] = ran(first_term(plan, me, *args, after()))

    def do_mixed(start, length):
        args = (plan, in_hbm(sums["u"]), second_t, "own_mixed", start, length, after())
        return ran(own_product(*args))

    def send_mixed(bufs, start, length, slot):
        arrived = send(hold(bufs, after(slot)))
        for k in range(count):
            if start <= chunks[k][0] < start + length:
                mixed[k] = (arrived, chunks[k][0] - start)

    def do_gate(k, slot, extra=()):
        arrived, inside = mixed[k]
        args = (hbm(arrived), inside, hbm(grad_u[k]), tokens, cotangent, first_t, sums["held"])
        *held, done = gate(plan, me, *args, *chunks[k], after(slot) + list(extra))
        sums["held"] = held
        ran(done)

    place = lax.axis_index("dp").astype(jnp.int32).reshape(1)
    state = []

    def split(slot):
        total = sums["first"].reshape(nloc * blk, blk)
        state[:] = ran(halves(place, total, after(slot)))
        state[1] = swap(state[1], 1, "dp", parts)

    def reduce(slot):
        state[:] = ran(quarters(place, *state, parts // 2, after(slot)))
        state[1:] = [swap(v, 2 * e, "dp", parts) for e, v in enumerate(state[1:], 1)]

    def add(slot):
        summed = ran(add_up(place, state[0], state[1:], after(slot)))
        state[:] = [summed] + [swap(summed, 2 * e, "dp", parts) for e in range(1, parts // 2)]

    def join(slot):
        mine = ran(join_parts(place, state, after(slot)))
        state[:] = [mine, swap(mine, 1, "dp", parts)]

    def finish(slot):
        state[:] = [ran(join_halves(place, *state[:2], after(slot) + state[2:]))]

    lead = 3
    for k in range(count):
        do_grad_z(k, k - lead)
        if k == min(lead, count) - 1:
            first_t, second, second_t = ran(
                prepare(plan, me, first_factor, second_factor, after())
            )
    for k in range(count):
        do_hidden(k, count + k - lead)
        do_kept(k)
    do_u(0)
    for k in range(count):
        do_grad_u(k, 2 * count + k - lead)
        if k + 1 < count:
            do_u(k + 1)
        if k == count - 3:
            do_u(k + 2)
            break
    for k in range(max(count - 2, 1), count):
        do_grad_u(k, 2 * count - 1)
    second_grad = lax.psum(sums["second"], "dp")
    late = do_mixed(size, rows - size) if count > 1 else None
    early = do_mixed(0, size)
    for k in range(count - 1):
        do_first(k)
    if count > 1:
        send_mixed(late, size, rows - size, 3 * count - 1)
    do_first(count - 1)
    split(None)
    reduce(None)
    send_mixed(early, 0, size, None)
    add(None)
    for k in range(1, count):
        do_gate(k, None, [second_grad] if k == count - 1 else [])
    join(None)
    do_gate(0, None)
    finish(None)
    first_grad = state[0].reshape(nloc, blk, blk)
    held = sums["held"]
    return (held[0], held[1], first_grad, second_grad)


def solution(mesh):
    return jax.shard_map(
        shards,
        mesh=mesh,
        in_specs=(P("dp", "mp"), P("dp", "mp"), P("mp", None, None), P("mp", None, None)),
        out_specs=(P("dp", "mp"), P("dp", "mp"), P("mp", None, None), P("mp", None, None)),
        check_vma=False,
    )
```

```python
import functools

import jax
import jax.numpy as jnp
from jax import lax
from jax.experimental import pallas as pl
from jax.experimental.pallas import tpu as pltpu
from jax.sharding import PartitionSpec as P

BF16, F32 = jnp.bfloat16, jnp.float32
SMEM = pl.BlockSpec(memory_space=pltpu.SMEM)
VMEM_LIMIT = 16 * 2**20
SPAN = 256
GROUP = 256


class Plan:
    def __init__(self, rows, nloc, blk, groups):
        self.rows, self.nloc, self.blk, self.groups = rows, nloc, blk, groups
        self.ratio = blk // (nloc * groups)
        self.piece = self.ratio * nloc
        self.wire = nloc * self.piece
        self.tile = GROUP // nloc
        self.ngroup = nloc * blk // GROUP
        self.span = min(SPAN, rows)


def iotas(size):
    return (
        lax.broadcasted_iota(jnp.int32, (size, size), 0),
        lax.broadcasted_iota(jnp.int32, (size, size), 1),
    )


def onehot(mask):
    return jnp.where(mask, 1.0, 0.0).astype(BF16)


def relative(plan, me):
    r, c = iotas(plan.blk)
    return onehot((r ^ c) == me * plan.piece)


def source_order(plan, me):
    r, c = iotas(plan.blk)
    nblk = plan.nloc * plan.groups
    return onehot(c == (r & (plan.ratio - 1)) * nblk + ((r // plan.ratio) ^ (me * plan.nloc)))


def regroup(plan, back):
    r, c = iotas(GROUP)
    if back:
        r, c = c, r
    return onehot(
        c
        == ((r & (plan.tile - 1)) // plan.ratio) * plan.piece
        + (r // plan.tile) * plan.ratio
        + (r & (plan.ratio - 1))
    )


def dot(a, b, dims):
    return lax.dot_general(a, b, (dims, ((), ())), preferred_element_type=F32)


NN, NT, TN = ((1,), (0,)), ((1,), (1,)), ((0,), (0,))


def sigmoid(x):
    return 0.5 * jnp.tanh(0.5 * x) + 0.5


def in_hbm(array):
    return pltpu.with_memory_space_constraint(array, pltpu.HBM)


def join(parts):
    return parts[0] if len(parts) == 1 else jnp.concatenate(parts, axis=0)


def scatter(plan, value, outs, block):
    piece = plan.piece
    at = slice(block * piece, (block + 1) * piece)
    for e in range(plan.groups):
        part = value[e * piece : (e + 1) * piece].astype(BF16)
        outs[e][at, :] = part


def gather(plan, refs, block):
    piece = plan.piece
    parts = []
    for ref in refs:
        part = ref[block * piece : (block + 1) * piece, :]
        parts.append(part if piece % 16 == 0 else part.astype(F32))
    return jnp.concatenate(parts, axis=0).astype(BF16)


def params(count=1):
    return pltpu.CompilerParams(
        dimension_semantics=("arbitrary",) * count, vmem_limit_bytes=VMEM_LIMIT
    )


def cost(flops, moved):
    return pl.CostEstimate(flops=int(flops), bytes_accessed=int(moved), transcendentals=0)


def sends(plan, size, step):
    shapes = [jax.ShapeDtypeStruct((plan.wire, size), BF16)] * plan.groups
    return shapes, arrivals(plan, size, step)


def arrivals(plan, size, step, inside=0):
    at = inside // size
    return [pl.BlockSpec((step * plan.piece, size), lambda i: (i, at))] * plan.groups


def call(kernel, args, in_specs, after=(), into=None, **kwargs):
    count = len(args)
    if into is not None:
        after = [into, *after]
        kwargs["input_output_aliases"] = {count: 0}
    extra = len(after)

    def body(*refs):
        kernel(*refs[:count], *refs[count + extra :])

    return pl.pallas_call(
        body,
        in_specs=list(in_specs) + [pl.BlockSpec(memory_space=pl.ANY)] * extra,
        **kwargs,
    )(*args, *after)


def hold(arrays, after):
    count = len(arrays)
    anywhere = pl.BlockSpec(memory_space=pl.ANY)
    return pl.pallas_call(
        lambda *refs: None,
        out_shape=[pltpu.HBM(a.shape, a.dtype) for a in arrays],
        in_specs=[anywhere] * (count + len(after)),
        out_specs=[anywhere] * count,
        input_output_aliases={i: i for i in range(count)},
        name="hold",
    )(*arrays, *after)


def prepare(plan, me, first, second, after=()):
    def kernel(me_ref, f_ref, s_ref, ft_ref, s_out, st_out):
        rel = relative(plan, me_ref[0])
        order = source_order(plan, me_ref[0])
        for i in range(plan.nloc):
            ft_ref[i] = dot(rel, f_ref[i], NT).astype(BF16)
            rows = dot(order, s_ref[i], NN).astype(BF16)
            s_out[i] = dot(rows, rel, NN).astype(BF16)
            st_out[i] = dot(rel, rows, NT).astype(BF16)

    shape = jax.ShapeDtypeStruct(first.shape, BF16)
    return call(
        kernel,
        (me, first, second),
        [SMEM] + [pl.BlockSpec(memory_space=pltpu.VMEM)] * 2,
        after,
        out_shape=[shape] * 3,
        out_specs=[pl.BlockSpec(memory_space=pltpu.VMEM)] * 3,
        compiler_params=pltpu.CompilerParams(vmem_limit_bytes=VMEM_LIMIT),
        cost_estimate=cost(8 * plan.nloc * plan.blk**3, 5 * first.size * 2),
        name="prepare_factors",
    )


def send_grad_z(plan, me, tokens, cotangent, start, size, after=()):
    step = min(8, plan.nloc)
    shapes, specs = sends(plan, size, step)

    def kernel(me_ref, x_ref, g_ref, *outs):
        rel = relative(plan, me_ref[0])
        for i in range(step):
            cols = slice(i * plan.blk, (i + 1) * plan.blk)
            xf = x_ref[:, cols].astype(F32)
            silu = xf * sigmoid(xf)
            grad_z = (g_ref[:, cols].astype(F32) * silu).astype(BF16)
            scatter(plan, dot(rel, grad_z, NT), outs, i)

    block = pl.BlockSpec((size, step * plan.blk), lambda i: (start // size, i))
    return call(
        kernel,
        (me, tokens, cotangent),
        [SMEM, block, block],
        after,
        grid=(plan.nloc // step,),
        out_shape=shapes,
        out_specs=specs,
        compiler_params=params(),
        cost_estimate=cost(2 * size * plan.nloc * plan.blk**2, 6 * size * plan.nloc * plan.blk),
        name="send_grad_z",
    )


def send_hidden(plan, tokens, first_t, start, size, after=()):
    step = min(8, plan.nloc)
    shapes, specs = sends(plan, size, step)

    def kernel(x_ref, w_ref, *outs):
        for i in range(step):
            cols = slice(i * plan.blk, (i + 1) * plan.blk)
            scatter(plan, dot(w_ref[i], x_ref[:, cols], NT), outs, i)

    return call(
        kernel,
        (tokens, first_t),
        [
            pl.BlockSpec((size, step * plan.blk), lambda i: (start // size, i)),
            pl.BlockSpec((step, plan.blk, plan.blk), lambda i: (i, 0, 0)),
        ],
        after,
        grid=(plan.nloc // step,),
        out_shape=shapes,
        out_specs=specs,
        compiler_params=params(),
        cost_estimate=cost(2 * size * plan.nloc * plan.blk**2, 4 * size * plan.nloc * plan.blk),
        name="send_hidden",
    )


def to_blocks(plan, refs, out):
    matrix = regroup(plan, False)
    for g in range(plan.ngroup):
        begin, parts = g * GROUP, []
        while begin < (g + 1) * GROUP:
            e, inside = begin // plan.wire, begin % plan.wire
            take = min(plan.wire - inside, (g + 1) * GROUP - begin)
            parts.append(refs[e][inside : inside + take, :])
            begin += take
        moved = dot(matrix, join(parts), NN).astype(BF16)
        for j in range(plan.nloc):
            out[j, g * plan.tile : (g + 1) * plan.tile, :] = moved[
                j * plan.tile : (j + 1) * plan.tile
            ]


def from_blocks(plan, held, outs):
    matrix = regroup(plan, True)
    for g in range(plan.ngroup):
        rows = join([held[j, g * plan.tile : (g + 1) * plan.tile, :] for j in range(plan.nloc)])
        moved = dot(matrix, rows, NN).astype(BF16)
        begin = g * GROUP
        while begin < (g + 1) * GROUP:
            e, inside = begin // plan.wire, begin % plan.wire
            take = min(plan.wire - inside, (g + 1) * GROUP - begin)
            part = moved[begin - g * GROUP : begin - g * GROUP + take]
            at = slice(inside, inside + take)
            outs[e][at, :] = part
            begin += take


def whole_spec(shape):
    return pl.BlockSpec(shape, lambda i: (0,) * len(shape))


def own_grad_mixed(plan, arrived, size, after=()):
    count = len(arrived)
    kept = (plan.nloc, plan.blk, size)

    def kernel(*refs):
        to_blocks(plan, refs[:count], refs[count])

    return call(
        kernel,
        list(arrived),
        arrivals(plan, size, plan.nloc),
        after,
        grid=(1,),
        out_shape=pltpu.VMEM(kept, BF16),
        out_specs=whole_spec(kept),
        compiler_params=params(),
        cost_estimate=cost(
            4 * size * plan.nloc * plan.blk**2, 4 * size * plan.nloc * plan.blk
        ),
        name="own_grad_mixed",
    )


def own_u(plan, me, arrived, grad_mixed, total, into, start, size, scale, after=()):
    count = len(arrived)
    kept = (plan.nloc, plan.blk, size)
    square = (plan.nloc, plan.blk, plan.blk)
    extra = [] if total is None else [total]

    def kernel(*refs):
        me_ref, ins, g_ref = refs[0], refs[1 : 1 + count], refs[1 + count]
        u_ref, sum_ref = refs[-2:]
        to_blocks(plan, ins, u_ref)
        if scale is not None:
            rel, order = relative(plan, me_ref[0]), source_order(plan, me_ref[0])
        for j in range(plan.nloc):
            term = dot(u_ref[j], g_ref[j], NT)
            if extra:
                term = term + refs[2 + count][j]
            if scale is not None:
                term = dot(order, (term * scale).astype(BF16), TN).astype(BF16)
                term = dot(term, rel, NN)
            sum_ref[j] = term

    return call(
        kernel,
        [me] + list(arrived) + [grad_mixed] + extra,
        [SMEM]
        + arrivals(plan, size, plan.nloc)
        + [whole_spec(kept)]
        + [whole_spec(square)] * len(extra),
        after,
        into,
        grid=(1,),
        out_shape=[
            pltpu.HBM((plan.nloc, plan.blk, plan.rows), BF16),
            jax.ShapeDtypeStruct(square, F32),
        ],
        out_specs=[
            pl.BlockSpec(kept, lambda i: (0, 0, start // size)),
            whole_spec(square),
        ],
        compiler_params=params(),
        cost_estimate=cost(
            6 * size * plan.nloc * plan.blk**2, 6 * size * plan.nloc * plan.blk
        ),
        name="own_u",
    )


def own_product(plan, u, factor, name, start, size, after=()):
    span = plan.span
    shapes, _ = sends(plan, size, plan.nloc)
    shape = (plan.nloc, plan.blk, span)

    def kernel(u_ref, w_ref, *refs):
        outs, held = refs[:-1], refs[-1]
        for j in range(plan.nloc):
            held[j] = dot(w_ref[j], u_ref[j], NN).astype(BF16)
        from_blocks(plan, held, outs)

    return call(
        kernel,
        (u, in_hbm(factor)),
        [pl.BlockSpec(shape, lambda t: (0, 0, t + start // span)), whole_spec(factor.shape)],
        after,
        grid=(size // span,),
        out_shape=shapes,
        out_specs=[pl.BlockSpec((plan.wire, span), lambda t: (0, t))] * plan.groups,
        scratch_shapes=[pltpu.VMEM(shape, BF16)],
        compiler_params=params(),
        cost_estimate=cost(
            6 * size * plan.nloc * plan.blk**2, 4 * size * plan.nloc * plan.blk
        ),
        name=name,
    )


def first_term(plan, me, arrived, tokens, total, start, size, scale, after=()):
    count = len(arrived)
    step = min(8, plan.nloc)
    square = pl.BlockSpec((step, plan.blk, plan.blk), lambda i: (i, 0, 0))
    extra = [] if total is None else [total]

    def kernel(*refs):
        me_ref, ins, x_ref, sum_ref = refs[0], refs[1 : 1 + count], refs[1 + count], refs[-1]
        rel = relative(plan, me_ref[0])
        for i in range(step):
            cols = slice(i * plan.blk, (i + 1) * plan.blk)
            term = dot(gather(plan, ins, i), x_ref[:, cols], NN)
            if extra:
                term = term + refs[2 + count][i]
            if scale is not None:
                term = dot((term * scale).astype(BF16), rel, TN)
            sum_ref[i] = term.astype(sum_ref.dtype)

    return call(
        kernel,
        [me] + list(arrived) + [tokens] + extra,
        [SMEM]
        + arrivals(plan, size, step)
        + [pl.BlockSpec((size, step * plan.blk), lambda i: (start // size, i))]
        + [square] * len(extra),
        after,
        grid=(plan.nloc // step,),
        out_shape=jax.ShapeDtypeStruct(
            (plan.nloc, plan.blk, plan.blk), F32 if scale is None else BF16
        ),
        out_specs=square,
        compiler_params=params(),
        cost_estimate=cost(2 * size * plan.nloc * plan.blk**2, 4 * size * plan.nloc * plan.blk),
        name="first_term",
    )


def gate(plan, me, mixed, inside, grads, tokens, cotangent, first_t, held, start, size, after=()):
    count = len(mixed)
    step = min(8, plan.nloc)
    extra = [] if held is None else list(held)

    def kernel(*refs):
        me_ref, zs, hs = refs[0], refs[1 : 1 + count], refs[1 + count : 1 + 2 * count]
        x_ref, g_ref, w_ref = refs[1 + 2 * count : 4 + 2 * count]
        out_ref, grad_ref, done_ref = refs[-3:]
        done_ref[...] = jnp.zeros_like(done_ref)
        rel = relative(plan, me_ref[0])
        for i in range(step):
            cols = slice(i * plan.blk, (i + 1) * plan.blk)
            zf = dot(gather(plan, zs, i), rel, TN)
            back = dot(gather(plan, hs, i), w_ref[i], TN)
            xf = x_ref[:, cols].astype(F32)
            gf = g_ref[:, cols].astype(F32)
            sig = sigmoid(xf)
            silu = xf * sig
            out_ref[:, cols] = (zf * silu).astype(BF16)
            gate_grad = (gf * zf * (sig + silu * (1.0 - sig))).astype(BF16)
            grad_ref[:, cols] = (back + gate_grad.astype(F32)).astype(BF16)

    block = pl.BlockSpec((size, step * plan.blk), lambda i: (start // size, i))
    shape = pltpu.HBM(tokens.shape, BF16)
    before = 4 + 2 * count
    return call(
        kernel,
        [me] + list(mixed) + list(grads) + [tokens, cotangent, in_hbm(first_t)] + extra,
        [SMEM]
        + arrivals(plan, size, step, inside)
        + arrivals(plan, size, step)
        + [block, block, pl.BlockSpec((step, plan.blk, plan.blk), lambda i: (i, 0, 0))]
        + [pl.BlockSpec(memory_space=pl.ANY)] * len(extra),
        after,
        grid=(plan.nloc // step,),
        out_shape=[shape, shape, jax.ShapeDtypeStruct((8, 128), F32)],
        out_specs=[block, block, whole_spec((8, 128))],
        input_output_aliases={before: 0, before + 1: 1} if extra else {},
        compiler_params=params(),
        cost_estimate=cost(
            4 * size * plan.nloc * plan.blk**2, 12 * size * plan.nloc * plan.blk
        ),
        name="gate",
    )


def reorder(kernel, args, shapes, name, after=()):
    vmem = pl.BlockSpec(memory_space=pltpu.VMEM)
    moved = sum(a.size for a in args) * 2
    return call(
        kernel,
        args,
        [SMEM] + [vmem] * (len(args) - 1),
        after,
        out_shape=shapes,
        out_specs=[vmem] * len(shapes),
        compiler_params=pltpu.CompilerParams(vmem_limit_bytes=VMEM_LIMIT),
        cost_estimate=cost(moved, 2 * moved),
        name=name,
    )


def halves(place, total, after=()):
    rows, cols = total.shape
    half = rows // 2

    def kernel(place_ref, t_ref, keep_ref, send_ref):
        side = place_ref[0] & 1
        keep_ref[...] = t_ref[pl.ds(pl.multiple_of(side * half, half), half), :]
        send_ref[...] = t_ref[pl.ds(pl.multiple_of((1 - side) * half, half), half), :]

    return reorder(
        kernel, (place, total), [jax.ShapeDtypeStruct((half, cols), BF16)] * 2, "halves", after
    )


def quarters(place, keep, got, count, after=()):
    rows, cols = keep.shape
    part = rows // count

    def kernel(place_ref, a_ref, b_ref, *outs):
        for e in range(count):
            at = pl.multiple_of(((place_ref[0] >> 1) ^ e) * part, part)
            value = a_ref[pl.ds(at, part), :].astype(F32) + b_ref[pl.ds(at, part), :].astype(F32)
            outs[e][...] = value.astype(outs[e].dtype)

    shapes = [jax.ShapeDtypeStruct((part, cols), BF16 if e else F32) for e in range(count)]
    return reorder(kernel, (place, keep, got), shapes, "quarters", after)


def add_up(place, own, others, after=()):
    def kernel(place_ref, own_ref, *refs):
        value = own_ref[...]
        for ref in refs[:-1]:
            value = value + ref[...].astype(F32)
        refs[-1][...] = value.astype(BF16)

    shape = jax.ShapeDtypeStruct(own.shape, BF16)
    return reorder(kernel, (place, own, *others), [shape], "add_up", after)[0]


def join_parts(place, parts, after=()):
    count = len(parts)
    part, cols = parts[0].shape

    def kernel(place_ref, *refs):
        for e in range(count):
            at = pl.multiple_of(((place_ref[0] >> 1) ^ e) * part, part)
            refs[-1][pl.ds(at, part), :] = refs[e][...]

    shape = jax.ShapeDtypeStruct((part * count, cols), BF16)
    return reorder(kernel, (place, *parts), [shape], "join_parts", after)[0]


def join_halves(place, mine, other, after=()):
    half, cols = mine.shape

    def kernel(place_ref, m_ref, o_ref, out_ref):
        side = place_ref[0] & 1
        out_ref[pl.ds(pl.multiple_of(side * half, half), half), :] = m_ref[...].astype(F32)
        out_ref[pl.ds(pl.multiple_of((1 - side) * half, half), half), :] = o_ref[...].astype(F32)

    shape = pltpu.HBM((2 * half, cols), F32)
    return reorder(kernel, (place, mine, other), [shape], "join_halves", after)[0]


def swap(value, by, axis, size):
    return lax.ppermute(value, axis, [(i, i ^ by) for i in range(size)])


def shards(tokens, cotangent, first_factor, second_factor):
    nloc, blk, _ = first_factor.shape
    plan = Plan(tokens.shape[0], nloc, blk, lax.axis_size("mp"))
    rows, parts = plan.rows, lax.axis_size("dp")
    size = plan.span
    chunks = [(start, size) for start in range(0, rows, size)]
    count = len(chunks)
    me = lax.axis_index("mp").astype(jnp.int32).reshape(1)
    scale = float((rows * parts) ** -0.5)
    tokens = pltpu.with_memory_space_constraint(tokens, pltpu.HBM)
    cotangent = pltpu.with_memory_space_constraint(cotangent, pltpu.HBM)
    crossed = []
    order = []

    def after(slot=None):
        found = [] if slot is None or slot < 0 else list(crossed[slot])
        return found + order[-1:]

    def ran(result):
        order.append(result[0] if isinstance(result, (list, tuple)) else result)
        return result

    def send(bufs):
        ran(bufs)
        arrived = [bufs[0]]
        arrived += [swap(v, e, "mp", plan.groups) for e, v in enumerate(bufs[1:], 1)]
        crossed.append(arrived[2:])
        return arrived

    def hbm(arrays):
        return [pltpu.with_memory_space_constraint(a, pltpu.HBM) for a in arrays]

    grad_z, hidden, kept, grad_u, mixed = [], [], [], [], {}
    sums = dict(first=None, second=None, held=None, u=None)
    last = [None] * (count - 1) + [scale]

    def do_grad_z(k, slot):
        grad_z.append(send(send_grad_z(plan, me, tokens, cotangent, *chunks[k], after(slot))))

    def do_hidden(k, slot):
        hidden.append(send(send_hidden(plan, tokens, first_t, *chunks[k], after(slot))))

    def do_kept(k):
        kept.append(ran(own_grad_mixed(plan, grad_z[k], chunks[k][1], after())))

    def do_grad_u(k, slot):
        args = (plan, kept[k], second, "own_grad_u", 0, size, after(slot))
        grad_u.append(send(own_product(*args)))

    def do_u(k):
        args = (hidden[k], kept[k], sums["second"], sums["u"], *chunks[k], last[k], after())
        sums["u"], sums["second"] = own_u(plan, me, *args)
        ran(sums["second"])

    def do_first(k):
        args = (hbm(grad_u[k]), tokens, sums["first"], *chunks[k], last[k])
        sums["first"] = ran(first_term(plan, me, *args, after()))

    def do_mixed(start, length):
        args = (plan, in_hbm(sums["u"]), second_t, "own_mixed", start, length, after())
        return ran(own_product(*args))

    def send_mixed(bufs, start, length, slot):
        arrived = send(hold(bufs, after(slot)))
        for k in range(count):
            if start <= chunks[k][0] < start + length:
                mixed[k] = (arrived, chunks[k][0] - start)

    def do_gate(k, slot, extra=()):
        arrived, inside = mixed[k]
        args = (hbm(arrived), inside, hbm(grad_u[k]), tokens, cotangent, first_t, sums["held"])
        *held, done = gate(plan, me, *args, *chunks[k], after(slot) + list(extra))
        sums["held"] = held
        ran(done)

    place = lax.axis_index("dp").astype(jnp.int32).reshape(1)
    state = []

    def split(slot):
        total = sums["first"].reshape(nloc * blk, blk)
        state[:] = ran(halves(place, total, after(slot)))
        state[1] = swap(state[1], 1, "dp", parts)

    def reduce(slot):
        state[:] = ran(quarters(place, *state, parts // 2, after(slot)))
        state[1:] = [swap(v, 2 * e, "dp", parts) for e, v in enumerate(state[1:], 1)]

    def add(slot):
        summed = ran(add_up(place, state[0], state[1:], after(slot)))
        state[:] = [summed] + [swap(summed, 2 * e, "dp", parts) for e in range(1, parts // 2)]

    def join(slot):
        mine = ran(join_parts(place, state, after(slot)))
        state[:] = [mine, swap(mine, 1, "dp", parts)]

    def finish(slot):
        state[:] = [ran(join_halves(place, *state[:2], after(slot) + state[2:]))]

    lead = 3
    for k in range(count):
        do_grad_z(k, k - lead)
        if k == min(lead, count) - 1:
            first_t, second, second_t = ran(
                prepare(plan, me, first_factor, second_factor, after())
            )
    for k in range(count):
        do_hidden(k, count + k - lead)
        do_kept(k)
    do_u(0)
    for k in range(count):
        do_grad_u(k, 2 * count + k - lead)
        if k + 1 < count:
            do_u(k + 1)
        if k == count - 3:
            do_u(k + 2)
            break
    for k in range(max(count - 2, 1), count):
        do_grad_u(k, 2 * count - 1)
    second_grad = lax.psum(sums["second"], "dp")
    late = do_mixed(size, rows - size) if count > 1 else None
    early = do_mixed(0, size)
    for k in range(count - 1):
        do_first(k)
    if count > 1:
        send_mixed(late, size, rows - size, 3 * count - 1)
    do_first(count - 1)
    split(None)
    reduce(None)
    send_mixed(early, 0, size, None)
    add(None)
    for k in range(1, count):
        do_gate(k, None, [second_grad] if k == count - 1 else [])
    join(None)
    do_gate(0, None)
    finish(None)
    first_grad = state[0].reshape(nloc, blk, blk)
    held = sums["held"]
    return (held[0], held[1], first_grad, second_grad)


def solution(mesh):
    return jax.shard_map(
        shards,
        mesh=mesh,
        in_specs=(P("dp", "mp"), P("dp", "mp"), P("mp", None, None), P("mp", None, None)),
        out_specs=(P("dp", "mp"), P("dp", "mp"), P("mp", None, None), P("mp", None, None)),
        check_vma=False,
    )
```
